32 devices in a mesh: patch: 16 (over z, y, x), head: 2 (over core).
Axes of the slice: x: 2, y: 2, z: 4, core: 2. Of those that a mesh axis runs over, the one named last changes fastest.
Arguments:
- hidden: bfloat16 [2, 3072, 3072], P(None, 'patch', 'head'), may hold values from -6 to 6
- stale_kv: bfloat16 [2, 3072, 3072], P(None, 'patch', 'head'), may hold values from -8 to 8
- modulation: float32 [2, 2, 3072], replicated, may hold values from -3 to 3
- attn_gate: float32 [2, 3072], P(None, 'head'), may hold values from 0.5 to 2
- w_qkv: bfloat16 [3072, 3, 3072], P(None, None, 'head'), may hold values from -2 to 2
- w_out: bfloat16 [3072, 3072], P('head'), may hold values from -0.109375 to 0.109375
Outputs:
- updated: bfloat16 [2, 3072, 3072], P(None, 'patch', 'head')
The draws below stay inside these ranges and needn't reach their ends.
All inputs are finite; a program needn't handle non-finite values.
Results may differ from the reference program's by a relative error of at most 0.019.
Values may be sent and summed in bfloat16 or wider, within the bound.
A program may use at most 192 MiB of HBM per device.

```python
import jax
import jax.numpy as jnp
from jax import lax

D = 3072
HEADS = 24
HEAD_DIM = 128
TOK_DEV = 192
STEPS = 2
TOKENS = 3072
N_PATCH = 16


def draw_hidden(key, part):
    key = jax.random.fold_in(key, 11)
    drawn = jax.random.normal(key, (STEPS, TOKENS, D), jnp.float32)
    return jnp.clip(drawn, -6.0, 6.0).astype(jnp.bfloat16)


def draw_modulation(key, part):
    key = jax.random.fold_in(key, 37)
    drawn = 0.5 * jax.random.normal(key, (STEPS, 2, D), jnp.float32)
    return jnp.clip(drawn, -3.0, 3.0).astype(jnp.float32)


def draw_w_qkv(key, part):
    key = jax.random.fold_in(key, 23)
    inverse_root = D ** (-0.5)
    normal_part = jnp.clip(jax.random.normal(key, (D, 3, D), jnp.float32), -6.0, 6.0)
    column_scale = jnp.array([1.6, 1.6, 1.0], jnp.float32) * inverse_root
    drawn = normal_part * column_scale[None, :, None]
    return jnp.clip(drawn, -2.0, 2.0).astype(jnp.bfloat16)


def level_of(key, extent, cuts, low, largest):
    loudness, own = 1.0, jax.random.fold_in(key, 6)
    for dim, shards_of in cuts:
        heights = jnp.exp(jax.random.uniform(jax.random.fold_in(own, dim), (shards_of,), jnp.float32, low / len(cuts), largest / len(cuts)))
        loudness = loudness * jnp.repeat(heights, extent[dim] // shards_of).reshape([-1 if axis == dim else 1 for axis in range(len(extent))])
    return loudness


def scatter_about(own_key, dims, width, most, pieces=(), kind=jnp.bfloat16):
    loudness = level_of(own_key, dims, pieces, -0.22, 0.18) if pieces else 1.0
    entries = jax.random.normal(own_key, dims, jnp.float32) * width * loudness
    return jnp.minimum(jnp.maximum(entries, -most), most).astype(kind)


def setup_inputs(seed: int = 0) -> dict:
    key_of = jax.random.split(jax.random.key(seed), 7)
    return {
        "hidden": draw_hidden(jax.random.fold_in(key_of[6], 71), 0),
        "stale_kv": scatter_about(key_of[1], (2, TOKENS, D), 1.5, 8.0, ((1, 16), (2, 2))),
        "modulation": draw_modulation(jax.random.fold_in(key_of[6], 71), 0),
        "attn_gate": jnp.clip(0.5 + 1.5 * jax.random.uniform(key_of[3], (STEPS, D), jnp.float32) ** level_of(key_of[3], (STEPS, D), ((1, 2),), -0.2, 0.2), 0.5, 2.0),
        "w_qkv": draw_w_qkv(jax.random.fold_in(key_of[6], 71), 0),
        "w_out": scatter_about(key_of[5], (D, D), D ** -0.5, 0.109375, ((0, 2),)),
    }


def layer_norm(values_in):
    mean_value = lax.optimization_barrier(jnp.mean(values_in, axis=-1, keepdims=True))
    centred = values_in - mean_value
    variance = lax.optimization_barrier(jnp.mean(centred * centred, axis=-1, keepdims=True))
    return centred * lax.rsqrt(variance + 1e-06)

def attend(queries, key_rows, value_rows):
    query_float = queries.astype(jnp.float32).reshape(TOK_DEV, HEADS, HEAD_DIM)
    key_float = key_rows.astype(jnp.float32).reshape(TOKENS, HEADS, HEAD_DIM)
    value_float = value_rows.astype(jnp.float32).reshape(TOKENS, HEADS, HEAD_DIM)
    scores = jnp.einsum('qhd,khd->qhk', query_float, key_float) * HEAD_DIM ** (-0.5)
    row_peak = lax.optimization_barrier(jnp.max(scores, axis=-1, keepdims=True))
    weights = lax.optimization_barrier(jnp.exp(scores - row_peak).astype(jnp.bfloat16))
    weights_float = weights.astype(jnp.float32)
    row_total = lax.optimization_barrier(jnp.sum(weights_float, axis=-1))
    weighted = jnp.einsum('qhk,khd->qhd', weights_float, value_float)
    return (weighted / row_total[..., None]).astype(jnp.bfloat16).reshape(TOK_DEV, D)

def reference(hidden, stale_kv, modulation, attn_gate, w_qkv, w_out):
    previous_keys = stale_kv[0]
    previous_values = stale_kv[1]
    results = []
    for step_index in range(STEPS):
        normed = layer_norm(hidden[step_index].astype(jnp.float32))
        normed = (normed * (1.0 + modulation[step_index, 1]) + modulation[step_index, 0]).astype(jnp.bfloat16)
        queries = jnp.dot(normed, w_qkv[:, 0, :], preferred_element_type=jnp.float32).astype(jnp.bfloat16)
        fresh_keys = jnp.dot(normed, w_qkv[:, 1, :], preferred_element_type=jnp.float32).astype(jnp.bfloat16)
        fresh_values = jnp.dot(normed, w_qkv[:, 2, :], preferred_element_type=jnp.float32).astype(jnp.bfloat16)

        def one_slab(slab_index, queries=queries, fresh_keys=fresh_keys, fresh_values=fresh_values, previous_keys=previous_keys, previous_values=previous_values):
            offset_row = (slab_index * TOK_DEV).astype(jnp.int32)
            zero_col = jnp.int32(0)
            own_keys = lax.dynamic_slice(fresh_keys, (offset_row, zero_col), (TOK_DEV, D))
            own_values = lax.dynamic_slice(fresh_values, (offset_row, zero_col), (TOK_DEV, D))
            key_rows = lax.dynamic_update_slice(previous_keys, own_keys, (offset_row, zero_col))
            value_rows = lax.dynamic_update_slice(previous_values, own_values, (offset_row, zero_col))
            slab_queries = lax.dynamic_slice(queries, (offset_row, zero_col), (TOK_DEV, D))
            return attend(slab_queries, key_rows, value_rows)
        attended = lax.map(one_slab, jnp.arange(N_PATCH, dtype=jnp.int32)).reshape(TOKENS, D)
        branch = jnp.dot(attended, w_out, preferred_element_type=jnp.float32)
        results.append((hidden[step_index].astype(jnp.float32) + attn_gate[step_index] * branch).astype(jnp.bfloat16))
        previous_keys = fresh_keys
        previous_values = fresh_values
    return jnp.stack(results)
```

```python
import functools
import math

import jax
import jax.numpy as jnp
from jax import lax
from jax.experimental import pallas as pl
from jax.experimental.pallas import tpu as pltpu
from jax.sharding import PartitionSpec as P

HEAD_DIM = 128
SCALE = HEAD_DIM ** (-0.5) * math.log2(math.e)


def layer_norm(values_in):
    mean_value = jnp.mean(values_in, axis=-1, keepdims=True)
    centred = values_in - mean_value
    variance = jnp.mean(centred * centred, axis=-1, keepdims=True)
    return centred * lax.rsqrt(variance + 1e-06)


def attend_kernel(ring, slab, q_ref, k_ref, v_ref, kf_ref, vf_ref, o_ref, kbuf, vbuf):
    mine = lax.rem(lax.axis_index("patch"), ring)
    group = q_ref.shape[0] // slab
    kbuf[...] = k_ref[:, 0]
    vbuf[...] = v_ref[:, 0]

    def one_slab(j, carry):
        rows = pl.ds(pl.multiple_of(j * slab, slab), slab)
        here = pl.ds(mine, 1)
        kbuf[here, rows] = kf_ref[rows][None]
        vbuf[here, rows] = vf_ref[rows][None]
        keys = kbuf[...].reshape(ring * group * slab, HEAD_DIM)
        values = vbuf[...].reshape(ring * group * slab, HEAD_DIM)
        scores = lax.dot_general(
            q_ref[rows], keys, (((1,), (1,)), ((), ())), preferred_element_type=jnp.float32
        )
        peak = jnp.max(scores, axis=-1, keepdims=True)
        weights = jnp.exp2((scores - peak) * SCALE)
        total = jnp.sum(weights, axis=-1, keepdims=True)
        summed = jnp.dot(weights.astype(jnp.bfloat16), values, preferred_element_type=jnp.float32)
        o_ref[rows] = (summed / total).astype(jnp.bfloat16)
        kbuf[here, rows] = k_ref[here, 0, rows]
        vbuf[here, rows] = v_ref[here, 0, rows]
        return carry

    lax.fori_loop(0, group, one_slab, 0)


def attend(ring, slab, queries, gathered, fresh_keys, fresh_values):
    rows, width = queries.shape
    heads = width // HEAD_DIM
    flat = pl.BlockSpec((rows, HEAD_DIM), lambda h: (0, h))
    return pl.pallas_call(
        functools.partial(attend_kernel, ring, slab),
        grid=(heads,),
        out_shape=jax.ShapeDtypeStruct((rows, width), jnp.bfloat16),
        in_specs=[
            flat,
            pl.BlockSpec((ring, 1, rows, HEAD_DIM), lambda h: (0, 0, 0, h)),
            pl.BlockSpec((ring, 1, rows, HEAD_DIM), lambda h: (0, 1, 0, h)),
            flat,
            flat,
        ],
        out_specs=flat,
        scratch_shapes=[
            pltpu.VMEM((ring, rows, HEAD_DIM), jnp.bfloat16),
            pltpu.VMEM((ring, rows, HEAD_DIM), jnp.bfloat16),
        ],
        compiler_params=pltpu.CompilerParams(vmem_limit_bytes=48 * 2**20),
        cost_estimate=pl.CostEstimate(
            flops=4 * rows * width * rows * ring,
            bytes_accessed=2 * width * rows * (2 * ring + 4),
            transcendentals=rows * rows * ring * heads,
        ),
    )(queries, gathered, gathered, fresh_keys, fresh_values)


def on_device(patches, hidden, stale_kv, modulation, attn_gate, w_qkv, w_out):
    steps, slab, width = hidden.shape
    group = math.gcd(width // HEAD_DIM, patches)
    ring = patches // group
    columns = [[g * ring + p for g in range(group)] for p in range(ring)]
    planes = [[g * ring + p for p in range(ring)] for g in range(group)]
    part = width // group

    def spread(rows):
        n = rows.shape[0]
        if group == 1:
            return rows
        split = rows.reshape(n, slab, group, part).transpose(2, 0, 1, 3)
        got = lax.all_to_all(split, "patch", 0, 0, axis_index_groups=columns, tiled=True)
        return got.transpose(1, 0, 2, 3).reshape(n, group * slab, part)

    def gather(rows):
        return lax.all_gather(rows, "patch", axis=0, axis_index_groups=planes)

    stale_all = gather(spread(stale_kv))
    full_rows = lax.all_gather(hidden, "head", axis=2, tiled=True)
    normed = layer_norm(full_rows.astype(jnp.float32))
    normed = (normed * (1.0 + modulation[:, 1][:, None]) + modulation[:, 0][:, None]).astype(
        jnp.bfloat16
    )
    projected = jnp.dot(
        normed.reshape(steps * slab, -1),
        w_qkv.reshape(w_qkv.shape[0], -1),
        preferred_element_type=jnp.float32,
    ).astype(jnp.bfloat16)
    projected = projected.reshape(steps, slab, 3, width).transpose(0, 2, 1, 3)
    q0, k0, v0, q1, k1, v1 = spread(projected.reshape(steps * 3, slab, width))
    fresh_all = gather(jnp.stack([k0, v0]))
    outs = jnp.stack(
        [attend(ring, slab, q0, stale_all, k0, v0), attend(ring, slab, q1, fresh_all, k1, v1)]
    )
    if group > 1:
        back = outs.reshape(steps, group, slab, part).transpose(1, 0, 2, 3)
        back = lax.all_to_all(back, "patch", 0, 0, axis_index_groups=columns, tiled=True)
        outs = back.transpose(1, 2, 0, 3).reshape(steps, slab, width)
    partial_out = jnp.dot(
        outs.reshape(steps * slab, width), w_out, preferred_element_type=jnp.float32
    )
    branch = lax.psum_scatter(
        partial_out.astype(jnp.bfloat16), "head", scatter_dimension=1, tiled=True
    ).astype(jnp.float32)
    gated = attn_gate[:, None] * branch.reshape(steps, slab, width)
    return (hidden.astype(jnp.float32) + gated).astype(jnp.bfloat16)


def solution(mesh):
    in_specs = (
        P(None, "patch", "head"),
        P(None, "patch", "head"),
        P(),
        P(None, "head"),
        P(None, None, "head"),
        P("head", None),
    )
    return jax.shard_map(
        functools.partial(on_device, mesh.shape["patch"]),
        mesh=mesh,
        in_specs=in_specs,
        out_specs=P(None, "patch", "head"),
        check_vma=False,
    )
```

```python
import functools
import math

import jax
import jax.numpy as jnp
from jax import lax
from jax.experimental import pallas as pl
from jax.experimental.pallas import tpu as pltpu
from jax.sharding import PartitionSpec as P

HEAD_DIM = 128
SCALE = HEAD_DIM ** (-0.5) * math.log2(math.e)


def layer_norm(values_in):
    mean_value = jnp.mean(values_in, axis=-1, keepdims=True)
    centred = values_in - mean_value
    variance = jnp.mean(centred * centred, axis=-1, keepdims=True)
    return centred * lax.rsqrt(variance + 1e-06)


def attend_kernel(ring, slab, q_ref, k_ref, v_ref, kf_ref, vf_ref, o_ref, kbuf, vbuf):
    mine = lax.rem(lax.axis_index("patch"), ring)
    group = q_ref.shape[0] // slab
    kbuf[...] = k_ref[:, 0]
    vbuf[...] = v_ref[:, 0]

    def one_slab(j, carry):
        rows = pl.ds(pl.multiple_of(j * slab, slab), slab)
        here = pl.ds(mine, 1)
        kbuf[here, rows] = kf_ref[rows][None]
        vbuf[here, rows] = vf_ref[rows][None]
        keys = kbuf[...].reshape(ring * group * slab, HEAD_DIM)
        values = vbuf[...].reshape(ring * group * slab, HEAD_DIM)
        scores = lax.dot_general(
            q_ref[rows], keys, (((1,), (1,)), ((), ())), preferred_element_type=jnp.float32
        )
        peak = jnp.max(scores, axis=-1, keepdims=True)
        weights = jnp.exp2((scores - peak) * SCALE)
        total = jnp.sum(weights, axis=-1, keepdims=True)
        summed = jnp.dot(weights.astype(jnp.bfloat16), values, preferred_element_type=jnp.float32)
        o_ref[rows] = (summed / total).astype(jnp.bfloat16)
        kbuf[here, rows] = k_ref[here, 0, rows]
        vbuf[here, rows] = v_ref[here, 0, rows]
        return carry

    lax.fori_loop(0, group, one_slab, 0)


def attend(ring, slab, queries, gathered, fresh_keys, fresh_values):
    rows, width = queries.shape
    heads = width // HEAD_DIM
    flat = pl.BlockSpec((rows, HEAD_DIM), lambda h: (0, h))
    return pl.pallas_call(
        functools.partial(attend_kernel, ring, slab),
        grid=(heads,),
        out_shape=jax.ShapeDtypeStruct((rows, width), jnp.bfloat16),
        in_specs=[
            flat,
            pl.BlockSpec((ring, 1, rows, HEAD_DIM), lambda h: (0, 0, 0, h)),
            pl.BlockSpec((ring, 1, rows, HEAD_DIM), lambda h: (0, 1, 0, h)),
            flat,
            flat,
        ],
        out_specs=flat,
        scratch_shapes=[
            pltpu.VMEM((ring, rows, HEAD_DIM), jnp.bfloat16),
            pltpu.VMEM((ring, rows, HEAD_DIM), jnp.bfloat16),
        ],
        compiler_params=pltpu.CompilerParams(vmem_limit_bytes=48 * 2**20),
        cost_estimate=pl.CostEstimate(
            flops=4 * rows * width * rows * ring,
            bytes_accessed=2 * width * rows * (2 * ring + 4),
            transcendentals=rows * rows * ring * heads,
        ),
    )(queries, gathered, gathered, fresh_keys, fresh_values)


K0, V0, Q0, Q1, K1, V1 = range(6)


def attend_step(query, fresh_k, fresh_v, own, others, kbuf, vbuf, store):
    group, slab, _ = kbuf.shape
    kbuf[...], vbuf[...] = own()

    def one_slot(j, carry):
        here = pl.ds(j, 1)
        kept_k, kept_v = kbuf[here], vbuf[here]
        kbuf[here] = fresh_k(here)
        vbuf[here] = fresh_v(here)
        rows = query(here).reshape(slab, HEAD_DIM)
        blocks = [(kbuf[...], vbuf[...])] + [other() for other in others]
        blocks = [[part.reshape(group * slab, HEAD_DIM) for part in block] for block in blocks]
        scores = [
            lax.dot_general(rows, k, (((1,), (1,)), ((), ())), preferred_element_type=jnp.float32)
            for k, _ in blocks
        ]
        peak = functools.reduce(
            jnp.maximum, [jnp.max(block, axis=-1, keepdims=True) for block in scores]
        )
        total, summed = 0.0, 0.0
        for block, (_, v) in zip(scores, blocks):
            weights = jnp.exp2((block - peak) * SCALE)
            total += jnp.sum(weights, axis=-1, keepdims=True)
            summed += jnp.dot(weights.astype(jnp.bfloat16), v, preferred_element_type=jnp.float32)
        store(here, (summed / total).astype(jnp.bfloat16)[None])
        kbuf[here] = kept_k
        vbuf[here] = kept_v
        return carry

    lax.fori_loop(0, group, one_slot, 0)


def exchange_kernel(
    ring, q_ref, k_ref, v_ref, stale_ref, att_ref,
    col, gath, st, out, kbuf, vbuf,
    z_send, z_recv, loc_sem, f_send, f_recv, o_send, o_recv, st_sem,
):
    me = lax.axis_index("patch")
    z, p = lax.div(me, ring), lax.rem(me, ring)
    _, group, slab, part = col.shape
    heads = part // HEAD_DIM

    def column_peer(d):
        return {"patch": lax.rem(z + d + group, group) * ring + p}

    def plane_peer(e):
        return {"patch": z * ring + lax.rem(p + e, ring)}

    barrier = pltpu.get_barrier_semaphore()
    for d in range(1, group):
        pl.semaphore_signal(barrier, inc=1, device_id=column_peer(d), device_id_type=pl.DeviceIdType.MESH)
    for e in range(1, ring):
        pl.semaphore_signal(barrier, inc=1, device_id=plane_peer(e), device_id_type=pl.DeviceIdType.MESH)
    pl.semaphore_wait(barrier, group + ring - 2)

    sources = {K0: (k_ref, 0), V0: (v_ref, 0), Q0: (q_ref, 0), Q1: (q_ref, 1), K1: (k_ref, 1), V1: (v_ref, 1)}

    def source(a, owner):
        ref, step = sources[a]
        columns = pl.ds(pl.multiple_of(owner * part, part), part)
        return ref.at[pl.ds(step * slab, slab), columns]

    moves = {}
    for a in range(6):
        moves[a, 0] = pltpu.make_async_copy(source(a, z), col.at[a, 0], loc_sem.at[a])
        moves[a, 0].start()
        for d in range(1, group):
            moves[a, d] = pltpu.make_async_remote_copy(
                src_ref=source(a, lax.rem(z + d, group)),
                dst_ref=col.at[a, d],
                send_sem=z_send.at[a, d],
                recv_sem=z_recv.at[a, d],
                device_id=column_peer(d),
                device_id_type=pl.DeviceIdType.MESH,
            )
            moves[a, d].start()
    stale_copy = pltpu.make_async_copy(stale_ref, st, st_sem)
    stale_copy.start()

    def arrive(a, d):
        if d == 0:
            moves[a, 0].wait()
        else:
            moves[a, d].wait_recv()

    forwards = []
    for d in range(group):
        for a in (K0, V0):
            arrive(a, d)
            for e in range(1, ring):
                forward = pltpu.make_async_remote_copy(
                    src_ref=col.at[a, d],
                    dst_ref=gath.at[a, e - 1, d],
                    send_sem=f_send.at[a, d, e],
                    recv_sem=f_recv.at[a, d, e],
                    device_id=plane_peer(e),
                    device_id_type=pl.DeviceIdType.MESH,
                )
                forward.start()
                forwards.append(forward)

    returns = []

    def run_step(step, query_a, key_a, value_a, own_of, others_of):
        for h in range(heads):
            lanes = pl.ds(h * HEAD_DIM, HEAD_DIM)

            def store(here, value):
                out[step, h, here] = value

            attend_step(
                lambda here: col[query_a, here, :, lanes],
                lambda here: col[key_a, here, :, lanes],
                lambda here: col[value_a, here, :, lanes],
                lambda: own_of(lanes),
                [lambda e=e: others_of(e, lanes) for e in range(1, ring)],
                kbuf, vbuf, store,
            )
            columns = pl.ds(pl.multiple_of(z * part + h * HEAD_DIM, HEAD_DIM), HEAD_DIM)
            landing = att_ref.at[pl.ds(step * slab, slab), columns]
            for j in range(group):
                if j == 0:
                    back = pltpu.make_async_copy(out.at[step, h, 0], landing, o_recv.at[step, h, 0])
                else:
                    back = pltpu.make_async_remote_copy(
                        src_ref=out.at[step, h, j],
                        dst_ref=landing,
                        send_sem=o_send.at[step, h, j],
                        recv_sem=o_recv.at[step, h, j],
                        device_id=column_peer(-j),
                        device_id_type=pl.DeviceIdType.MESH,
                    )
                back.start()
                returns.append(back)

    def stale_block(e, lanes):
        plane = pl.ds(lax.rem(p + e, ring), 1)
        shape = (group, slab, HEAD_DIM)
        return st[plane, :, 0, :, lanes].reshape(shape), st[plane, :, 1, :, lanes].reshape(shape)

    for d in range(group):
        arrive(Q0, d)
    stale_copy.wait()
    run_step(0, Q0, K0, V0, lambda lanes: stale_block(0, lanes), stale_block)
    for a in (Q1, K1, V1):
        for d in range(group):
            arrive(a, d)
    for forward in forwards:
        forward.wait_recv()
    run_step(
        1, Q1, K1, V1,
        lambda lanes: (col[K0, :, :, lanes], col[V0, :, :, lanes]),
        lambda e, lanes: (gath[0, e - 1, :, :, lanes], gath[1, e - 1, :, :, lanes]),
    )
    for back in returns:
        back.wait()
    for forward in forwards:
        forward.wait_send()
    for a in range(6):
        for d in range(1, group):
            moves[a, d].wait_send()


def exchange_attend(group, ring, slab, queries, keys, values, stale_all):
    rows, width = queries.shape
    part = width // group
    heads = part // HEAD_DIM
    dma = pltpu.SemaphoreType.DMA
    return pl.pallas_call(
        functools.partial(exchange_kernel, ring),
        out_shape=jax.ShapeDtypeStruct((rows, width), jnp.bfloat16),
        in_specs=[pl.BlockSpec(memory_space=pl.ANY)] * 4,
        out_specs=pl.BlockSpec(memory_space=pl.ANY),
        scratch_shapes=[
            pltpu.VMEM((6, group, slab, part), jnp.bfloat16),
            pltpu.VMEM((2, ring - 1, group, slab, part), jnp.bfloat16),
            pltpu.VMEM((ring, group, 2, slab, part), jnp.bfloat16),
            pltpu.VMEM((2, heads, group, slab, HEAD_DIM), jnp.bfloat16),
            pltpu.VMEM((group, slab, HEAD_DIM), jnp.bfloat16),
            pltpu.VMEM((group, slab, HEAD_DIM), jnp.bfloat16),
            dma((6, group)),
            dma((6, group)),
            dma((6,)),
            dma((2, group, ring)),
            dma((2, group, ring)),
            dma((2, heads, group)),
            dma((2, heads, group)),
            dma,
        ],
        compiler_params=pltpu.CompilerParams(
            collective_id=0, has_side_effects=True, vmem_limit_bytes=48 * 2**20
        ),
        cost_estimate=pl.CostEstimate(
            flops=4 * rows * width * slab * group * ring,
            bytes_accessed=2 * width * rows * 8,
            transcendentals=rows * slab * group * ring * width // HEAD_DIM,
        ),
    )(queries, keys, values, stale_all)


def on_columns(group, ring, hidden, stale_kv, modulation, attn_gate, w_qkv, w_out):
    steps, slab, width = hidden.shape
    part = width // group
    patches = group * ring
    planes = [[g * ring + p for p in range(ring)] for g in range(group)]
    z = lax.axis_index("patch") // ring

    def for_owner(d):
        return lax.dynamic_slice_in_dim(stale_kv, lax.rem(z + d, group) * part, part, 2)

    slots = [for_owner(0)]
    for d in range(1, group):
        shift = [(r, (r + d * ring) % patches) for r in range(patches)]
        slots.append(lax.ppermute(for_owner(d), "patch", shift))
    full_rows = lax.all_gather(hidden, "head", axis=2, tiled=True)
    slots, w_late = lax.optimization_barrier((jnp.stack(slots), w_qkv))
    stale_all = lax.all_gather(slots, "patch", axis=0, axis_index_groups=planes)
    normed = layer_norm(full_rows.astype(jnp.float32))
    normed = (normed * (1.0 + modulation[:, 1][:, None]) + modulation[:, 0][:, None]).astype(
        jnp.bfloat16
    )
    normed = normed.reshape(steps * slab, -1)

    def project(weights):
        return jnp.dot(normed, weights, preferred_element_type=jnp.float32).astype(jnp.bfloat16)

    keys, values, queries = project(w_qkv[:, 1]), project(w_qkv[:, 2]), project(w_late[:, 0])
    outs = exchange_attend(group, ring, slab, queries, keys, values, stale_all)
    return finish(outs, hidden, attn_gate, w_out)


def finish(outs, hidden, attn_gate, w_out):
    partial_out = jnp.dot(outs, w_out, preferred_element_type=jnp.float32)
    branch = lax.psum_scatter(
        partial_out.astype(jnp.bfloat16), "head", scatter_dimension=1, tiled=True
    ).astype(jnp.float32)
    gated = attn_gate[:, None] * branch.reshape(hidden.shape)
    return (hidden.astype(jnp.float32) + gated).astype(jnp.bfloat16)


def on_device(patches, hidden, stale_kv, modulation, attn_gate, w_qkv, w_out):
    steps, slab, width = hidden.shape
    group = math.gcd(width // HEAD_DIM, patches)
    ring = patches // group
    if group == 4 and ring == 4 and steps == 2:
        return on_columns(group, ring, hidden, stale_kv, modulation, attn_gate, w_qkv, w_out)
    columns = [[g * ring + p for g in range(group)] for p in range(ring)]
    planes = [[g * ring + p for p in range(ring)] for g in range(group)]
    part = width // group

    def spread(rows):
        n = rows.shape[0]
        if group == 1:
            return rows
        split = rows.reshape(n, slab, group, part).transpose(2, 0, 1, 3)
        got = lax.all_to_all(split, "patch", 0, 0, axis_index_groups=columns, tiled=True)
        return got.transpose(1, 0, 2, 3).reshape(n, group * slab, part)

    def gather(rows):
        return lax.all_gather(rows, "patch", axis=0, axis_index_groups=planes)

    stale_all = gather(spread(stale_kv))
    full_rows = lax.all_gather(hidden, "head", axis=2, tiled=True)
    normed = layer_norm(full_rows.astype(jnp.float32))
    normed = (normed * (1.0 + modulation[:, 1][:, None]) + modulation[:, 0][:, None]).astype(
        jnp.bfloat16
    )
    projected = jnp.dot(
        normed.reshape(steps * slab, -1),
        w_qkv.reshape(w_qkv.shape[0], -1),
        preferred_element_type=jnp.float32,
    ).astype(jnp.bfloat16)
    projected = projected.reshape(steps, slab, 3, width).transpose(0, 2, 1, 3)
    q0, k0, v0, q1, k1, v1 = spread(projected.reshape(steps * 3, slab, width))
    fresh_all = gather(jnp.stack([k0, v0]))
    outs = jnp.stack(
        [attend(ring, slab, q0, stale_all, k0, v0), attend(ring, slab, q1, fresh_all, k1, v1)]
    )
    if group > 1:
        back = outs.reshape(steps, group, slab, part).transpose(1, 0, 2, 3)
        back = lax.all_to_all(back, "patch", 0, 0, axis_index_groups=columns, tiled=True)
        outs = back.transpose(1, 2, 0, 3).reshape(steps, slab, width)
    return finish(outs.reshape(steps * slab, width), hidden, attn_gate, w_out)


def solution(mesh):
    in_specs = (
        P(None, "patch", "head"),
        P(None, "patch", "head"),
        P(),
        P(None, "head"),
        P(None, None, "head"),
        P("head", None),
    )
    return jax.shard_map(
        functools.partial(on_device, mesh.shape["patch"]),
        mesh=mesh,
        in_specs=in_specs,
        out_specs=P(None, "patch", "head"),
        check_vma=False,
    )
```

```python
import functools
import math

import jax
import jax.numpy as jnp
from jax import lax
from jax.experimental import pallas as pl
from jax.experimental.pallas import tpu as pltpu
from jax.sharding import PartitionSpec as P

HEAD_DIM = 128
SCALE = HEAD_DIM ** (-0.5) * math.log2(math.e)


def layer_norm(values_in):
    mean_value = jnp.mean(values_in, axis=-1, keepdims=True)
    centred = values_in - mean_value
    variance = jnp.mean(centred * centred, axis=-1, keepdims=True)
    return centred * lax.rsqrt(variance + 1e-06)


def attend_kernel(ring, slab, q_ref, k_ref, v_ref, kf_ref, vf_ref, o_ref, kbuf, vbuf):
    mine = lax.rem(lax.axis_index("patch"), ring)
    group = q_ref.shape[0] // slab
    kbuf[...] = k_ref[:, 0]
    vbuf[...] = v_ref[:, 0]

    def one_slab(j, carry):
        rows = pl.ds(pl.multiple_of(j * slab, slab), slab)
        here = pl.ds(mine, 1)
        kbuf[here, rows] = kf_ref[rows][None]
        vbuf[here, rows] = vf_ref[rows][None]
        keys = kbuf[...].reshape(ring * group * slab, HEAD_DIM)
        values = vbuf[...].reshape(ring * group * slab, HEAD_DIM)
        scores = lax.dot_general(
            q_ref[rows], keys, (((1,), (1,)), ((), ())), preferred_element_type=jnp.float32
        )
        peak = jnp.max(scores, axis=-1, keepdims=True)
        weights = jnp.exp2((scores - peak) * SCALE)
        total = jnp.sum(weights, axis=-1, keepdims=True)
        summed = jnp.dot(weights.astype(jnp.bfloat16), values, preferred_element_type=jnp.float32)
        o_ref[rows] = (summed / total).astype(jnp.bfloat16)
        kbuf[here, rows] = k_ref[here, 0, rows]
        vbuf[here, rows] = v_ref[here, 0, rows]
        return carry

    lax.fori_loop(0, group, one_slab, 0)


def attend(ring, slab, queries, gathered, fresh_keys, fresh_values):
    rows, width = queries.shape
    heads = width // HEAD_DIM
    flat = pl.BlockSpec((rows, HEAD_DIM), lambda h: (0, h))
    return pl.pallas_call(
        functools.partial(attend_kernel, ring, slab),
        grid=(heads,),
        out_shape=jax.ShapeDtypeStruct((rows, width), jnp.bfloat16),
        in_specs=[
            flat,
            pl.BlockSpec((ring, 1, rows, HEAD_DIM), lambda h: (0, 0, 0, h)),
            pl.BlockSpec((ring, 1, rows, HEAD_DIM), lambda h: (0, 1, 0, h)),
            flat,
            flat,
        ],
        out_specs=flat,
        scratch_shapes=[
            pltpu.VMEM((ring, rows, HEAD_DIM), jnp.bfloat16),
            pltpu.VMEM((ring, rows, HEAD_DIM), jnp.bfloat16),
        ],
        compiler_params=pltpu.CompilerParams(vmem_limit_bytes=48 * 2**20),
        cost_estimate=pl.CostEstimate(
            flops=4 * rows * width * rows * ring,
            bytes_accessed=2 * width * rows * (2 * ring + 4),
            transcendentals=rows * rows * ring * heads,
        ),
    )(queries, gathered, gathered, fresh_keys, fresh_values)


K0, V0, Q0, Q1, K1, V1, SK, SV = range(8)
PLACE = {K0: (1, 0), V0: (2, 0), Q0: (0, 0), Q1: (0, 1), K1: (1, 1), V1: (2, 1)}
PLANE = {SK: 0, SV: 1, K0: 2, V0: 3}
TILE = 256
MESH = pl.DeviceIdType.MESH


def attend_step(query, fresh_k, fresh_v, own, others, kbuf, vbuf, store):
    group, slab, _ = kbuf.shape
    kbuf[...], vbuf[...] = own()

    def one_slot(j, carry):
        here = pl.ds(j, 1)
        kept_k, kept_v = kbuf[here], vbuf[here]
        kbuf[here] = fresh_k(here)
        vbuf[here] = fresh_v(here)
        rows = query(here).reshape(slab, HEAD_DIM)
        blocks = [(kbuf[...], vbuf[...])] + [other() for other in others]
        blocks = [[part.reshape(group * slab, HEAD_DIM) for part in block] for block in blocks]
        scores = [
            lax.dot_general(rows, k, (((1,), (1,)), ((), ())), preferred_element_type=jnp.float32)
            for k, _ in blocks
        ]
        peak = functools.reduce(
            jnp.maximum, [jnp.max(block, axis=-1, keepdims=True) for block in scores]
        )
        total, summed = 0.0, 0.0
        for block, (_, v) in zip(scores, blocks):
            weights = jnp.exp2((block - peak) * SCALE)
            total += jnp.sum(weights, axis=-1, keepdims=True)
            summed += jnp.dot(weights.astype(jnp.bfloat16), v, preferred_element_type=jnp.float32)
        store(here, (summed / total).astype(jnp.bfloat16)[None])
        kbuf[here] = kept_k
        vbuf[here] = kept_v
        return carry

    lax.fori_loop(0, group, one_slot, 0)


def block_kernel(
    ring, hidden_ref, stale_ref, mod_ref, gate_ref, w_qkv_ref, w_out_ref, updated_ref,
    hid, normed, w_buf, proj, col, gath, out, att, w_out, give, take, kbuf, vbuf,
    z_send, z_recv, loc_sem, f_send, f_recv, o_send, o_recv, w_sem, w_out_sem, hid_sem, p_send, p_recv,
):
    me, core = lax.axis_index("patch"), lax.axis_index("head")
    z, p = lax.div(me, ring), lax.rem(me, ring)
    _, group, slab, part = col.shape
    _, steps, _, width = hid.shape
    heads = part // HEAD_DIM

    def column_peer(d):
        return {"patch": lax.rem(z + d + group, group) * ring + p}

    def plane_peer(e):
        return {"patch": z * ring + lax.rem(p + e, ring)}

    twin = {"head": 1 - core}
    barrier = pltpu.get_barrier_semaphore()
    greeted = [column_peer(d) for d in range(1, group)] + [plane_peer(e) for e in range(1, ring)]
    for peer in greeted + [twin]:
        pl.semaphore_signal(barrier, inc=1, device_id=peer, device_id_type=MESH)

    def weight_copy(n):
        which, half = (1, 2, 0)[n // 2], n % 2
        columns = pl.ds(half * (width // 2), width // 2)
        return pltpu.make_async_copy(
            w_qkv_ref.at[which, :, columns], w_buf.at[n % 2], w_sem.at[n % 2]
        )

    weight_copy(0).start()
    weight_copy(1).start()
    hid_own = pltpu.make_async_copy(hidden_ref, hid.at[core], hid_sem.at[0])
    hid_own.start()
    pl.semaphore_wait(barrier, group + ring - 1)
    hid_swap = pltpu.make_async_remote_copy(
        src_ref=hidden_ref, dst_ref=hid.at[core], send_sem=hid_sem.at[1], recv_sem=hid_sem.at[2],
        device_id=twin, device_id_type=MESH,
    )
    hid_swap.start()

    def source(a, owner):
        columns = pl.ds(pl.multiple_of(owner * part, part), part)
        if a in (SK, SV):
            return stale_ref.at[a - SK, :, columns]
        which, step = PLACE[a]
        return proj.at[which, pl.ds(step * slab, slab), columns]

    moves = {}

    def spread(arrays):
        for a in arrays:
            moves[a, 0] = pltpu.make_async_copy(source(a, z), col.at[a, 0], loc_sem.at[a])
            moves[a, 0].start()
        for d in range(1, group):
            for a in arrays:
                moves[a, d] = pltpu.make_async_remote_copy(
                    src_ref=source(a, lax.rem(z + d, group)),
                    dst_ref=col.at[a, d],
                    send_sem=z_send.at[a, d],
                    recv_sem=z_recv.at[a, d],
                    device_id=column_peer(d),
                    device_id_type=MESH,
                )
                moves[a, d].start()

    def arrive(a, d):
        if d == 0:
            moves[a, 0].wait()
        else:
            moves[a, d].wait_recv()

    forwards = {}

    def forward(a, d):
        arrive(a, d)
        for e in range(1, ring):
            slot = PLANE[a]
            forwards[a, d, e] = pltpu.make_async_remote_copy(
                src_ref=col.at[a, d],
                dst_ref=gath.at[slot, e - 1, d],
                send_sem=f_send.at[slot, d, e],
                recv_sem=f_recv.at[slot, d, e],
                device_id=plane_peer(e),
                device_id_type=MESH,
            )
            forwards[a, d, e].start()

    spread((SK, SV))
    forward(SK, 0)
    forward(SV, 0)
    hid_own.wait()
    hid_swap.wait_recv()

    block = slab // 4

    def norm_rows(n, carry):
        step = lax.div(n, 4)
        rows = pl.ds(pl.multiple_of(lax.rem(n, 4) * block, block), block)
        here = pl.ds(step, 1)
        halves = [hid[c, here, rows].reshape(block, width).astype(jnp.float32) for c in range(2)]
        count = 2 * width
        mean_value = sum(jnp.sum(half, axis=-1, keepdims=True) for half in halves) / count
        centred = [half - mean_value for half in halves]
        variance = sum(jnp.sum(half * half, axis=-1, keepdims=True) for half in centred) / count
        inverse = lax.rsqrt(variance + 1e-06)
        landing = pl.ds(pl.multiple_of(n * block, block), block)
        for c in range(2):
            lanes = pl.ds(c * width, width)
            shift = mod_ref[here, 0, lanes].reshape(1, width)
            scale = mod_ref[here, 1, lanes].reshape(1, width)
            value = centred[c] * inverse * (1.0 + scale) + shift
            normed[landing, lanes] = value.astype(jnp.bfloat16)
        return carry

    lax.fori_loop(0, 4 * steps, norm_rows, 0)

    def project(n):
        which, half = (1, 2, 0)[n // 2], n % 2
        weight_copy(n).wait()

        def tile(t, carry):
            lanes = pl.ds(pl.multiple_of(t * TILE, TILE), TILE)
            landing = pl.ds(pl.multiple_of(half * (width // 2) + t * TILE, TILE), TILE)
            value = jnp.dot(normed[...], w_buf[n % 2, :, lanes], preferred_element_type=jnp.float32)
            proj[which, :, landing] = value.astype(jnp.bfloat16)
            return carry

        lax.fori_loop(0, width // 2 // TILE, tile, 0)
        if n + 2 < 6:
            weight_copy(n + 2).start()

    project(0)
    project(1)
    spread((K0,))
    forward(SK, 1)
    forward(SV, 1)
    project(2)
    project(3)
    spread((V0,))
    forward(SK, 2)
    forward(SV, 2)
    project(4)
    project(5)
    spread((Q0,))
    spread((Q1,))
    spread((K1, V1))
    w_out_copies = []
    for side in range(2):
        half = 1 - core if side == 0 else core
        columns = pl.ds(pl.multiple_of(half * width, width), width)
        w_out_copies.append(
            pltpu.make_async_copy(w_out_ref.at[:, columns], w_out.at[side], w_out_sem.at[side])
        )
        w_out_copies[side].start()
    forward(SK, 3)
    forward(SV, 3)
    for d in range(group):
        forward(K0, d)
        forward(V0, d)

    returns = {}

    def run_step(step, query_a, key_a, value_a, past_k, past_v):
        for h in range(heads):
            lanes = pl.ds(h * HEAD_DIM, HEAD_DIM)

            def store(here, value):
                out[step, h, here] = value

            attend_step(
                lambda here: col[query_a, here, :, lanes],
                lambda here: col[key_a, here, :, lanes],
                lambda here: col[value_a, here, :, lanes],
                lambda: (col[past_k, :, :, lanes], col[past_v, :, :, lanes]),
                [
                    lambda e=e: (
                        gath[PLANE[past_k], e - 1, :, :, lanes],
                        gath[PLANE[past_v], e - 1, :, :, lanes],
                    )
                    for e in range(1, ring)
                ],
                kbuf, vbuf, store,
            )
            columns = pl.ds(pl.multiple_of(z * part + h * HEAD_DIM, HEAD_DIM), HEAD_DIM)
            landing = att.at[step, :, columns]
            for j in range(group):
                if j == 0:
                    back = pltpu.make_async_copy(out.at[step, h, 0], landing, o_recv.at[step, h, 0])
                else:
                    back = pltpu.make_async_remote_copy(
                        src_ref=out.at[step, h, j],
                        dst_ref=landing,
                        send_sem=o_send.at[step, h, j],
                        recv_sem=o_recv.at[step, h, j],
                        device_id=column_peer(-j),
                        device_id_type=MESH,
                    )
                back.start()
                returns[step, h, j] = back

    def wait_plane(arrays):
        for (a, _, _), copy in forwards.items():
            if a in arrays:
                copy.wait_recv()

    def branch_tile(step, side, t):
        lanes = pl.ds(pl.multiple_of(t * TILE, TILE), TILE)
        return lanes, jnp.dot(att[step], w_out[side, :, lanes], preferred_element_type=jnp.float32)

    def share(step):
        for back in [copy for key, copy in returns.items() if key[0] == step]:
            back.wait()

        def tile(t, carry):
            lanes, value = branch_tile(step, 0, t)
            give[step, :, lanes] = value.astype(jnp.bfloat16)
            return carry

        lax.fori_loop(0, width // TILE, tile, 0)
        copy = pltpu.make_async_remote_copy(
            src_ref=give.at[step], dst_ref=take.at[step],
            send_sem=p_send.at[step], recv_sem=p_recv.at[step],
            device_id=twin, device_id_type=MESH,
        )
        copy.start()
        return copy

    def update(step, copy):
        copy.wait_recv()

        def tile(t, carry):
            lanes, value = branch_tile(step, 1, t)
            value = value + take[step, :, lanes].astype(jnp.float32)
            before = hid[pl.ds(core, 1), step, :, lanes].reshape(slab, TILE).astype(jnp.float32)
            after = before + gate_ref[pl.ds(step, 1), lanes] * value
            updated_ref[step, :, lanes] = after.astype(jnp.bfloat16)
            return carry

        lax.fori_loop(0, width // TILE, tile, 0)

    for d in range(group):
        arrive(Q0, d)
    wait_plane((SK, SV))
    run_step(0, Q0, K0, V0, SK, SV)
    for a in (Q1, K1, V1):
        for d in range(group):
            arrive(a, d)
    wait_plane((K0, V0))
    run_step(1, Q1, K1, V1, K0, V0)
    for copy in w_out_copies:
        copy.wait()
    shares = [share(step) for step in range(steps)]
    for step in range(steps):
        update(step, shares[step])
    for copy in shares + [hid_swap] + list(forwards.values()):
        copy.wait_send()
    for (_, d), copy in moves.items():
        if d > 0:
            copy.wait_send()


def whole_block(group, ring, hidden, stale_kv, modulation, attn_gate, w_qkv, w_out):
    steps, slab, width = hidden.shape
    part = width // group
    heads = part // HEAD_DIM
    bf16, dma = jnp.bfloat16, pltpu.SemaphoreType.DMA
    vmem, anywhere = pl.BlockSpec(memory_space=pltpu.VMEM), pl.BlockSpec(memory_space=pl.ANY)
    return pl.pallas_call(
        functools.partial(block_kernel, ring),
        out_shape=jax.ShapeDtypeStruct(hidden.shape, bf16),
        in_specs=[anywhere, anywhere, vmem, vmem, anywhere, anywhere],
        out_specs=vmem,
        scratch_shapes=[
            pltpu.VMEM((2, steps, slab, width), bf16),
            pltpu.VMEM((steps * slab, 2 * width), bf16),
            pltpu.VMEM((2, 2 * width, width // 2), bf16),
            pltpu.VMEM((3, steps * slab, width), bf16),
            pltpu.VMEM((8, group, slab, part), bf16),
            pltpu.VMEM((4, ring - 1, group, slab, part), bf16),
            pltpu.VMEM((steps, heads, group, slab, HEAD_DIM), bf16),
            pltpu.VMEM((steps, slab, width), bf16),
            pltpu.VMEM((2, width, width), bf16),
            pltpu.VMEM((steps, slab, width), bf16),
            pltpu.VMEM((steps, slab, width), bf16),
            pltpu.VMEM((group, slab, HEAD_DIM), bf16),
            pltpu.VMEM((group, slab, HEAD_DIM), bf16),
            dma((8, group)),
            dma((8, group)),
            dma((8,)),
            dma((4, group, ring)),
            dma((4, group, ring)),
            dma((steps, heads, group)),
            dma((steps, heads, group)),
            dma((2,)),
            dma((2,)),
            dma((3,)),
            dma((steps,)),
            dma((steps,)),
        ],
        compiler_params=pltpu.CompilerParams(
            collective_id=0, has_side_effects=True, vmem_limit_bytes=60 * 2**20
        ),
        cost_estimate=pl.CostEstimate(
            flops=steps * slab * width * (16 * width + 4 * slab * group * ring),
            bytes_accessed=2 * width * (8 * width + 6 * steps * slab),
            transcendentals=steps * slab * slab * group * ring * width // HEAD_DIM,
        ),
    )(hidden, stale_kv, modulation, attn_gate, jnp.transpose(w_qkv, (1, 0, 2)), w_out)


def finish(outs, hidden, attn_gate, w_out):
    partial_out = jnp.dot(outs, w_out, preferred_element_type=jnp.float32)
    branch = lax.psum_scatter(
        partial_out.astype(jnp.bfloat16), "head", scatter_dimension=1, tiled=True
    ).astype(jnp.float32)
    gated = attn_gate[:, None] * branch.reshape(hidden.shape)
    return (hidden.astype(jnp.float32) + gated).astype(jnp.bfloat16)


def on_device(patches, hidden, stale_kv, modulation, attn_gate, w_qkv, w_out):
    steps, slab, width = hidden.shape
    group = math.gcd(width // HEAD_DIM, patches)
    ring = patches // group
    if group == 4 and ring == 4 and steps == 2 and w_out.shape[1] == 2 * width:
        return whole_block(group, ring, hidden, stale_kv, modulation, attn_gate, w_qkv, w_out)
    columns = [[g * ring + p for g in range(group)] for p in range(ring)]
    planes = [[g * ring + p for p in range(ring)] for g in range(group)]
    part = width // group

    def spread(rows):
        n = rows.shape[0]
        if group == 1:
            return rows
        split = rows.reshape(n, slab, group, part).transpose(2, 0, 1, 3)
        got = lax.all_to_all(split, "patch", 0, 0, axis_index_groups=columns, tiled=True)
        return got.transpose(1, 0, 2, 3).reshape(n, group * slab, part)

    def gather(rows):
        return lax.all_gather(rows, "patch", axis=0, axis_index_groups=planes)

    stale_all = gather(spread(stale_kv))
    full_rows = lax.all_gather(hidden, "head", axis=2, tiled=True)
    normed = layer_norm(full_rows.astype(jnp.float32))
    normed = (normed * (1.0 + modulation[:, 1][:, None]) + modulation[:, 0][:, None]).astype(
        jnp.bfloat16
    )
    projected = jnp.dot(
        normed.reshape(steps * slab, -1),
        w_qkv.reshape(w_qkv.shape[0], -1),
        preferred_element_type=jnp.float32,
    ).astype(jnp.bfloat16)
    projected = projected.reshape(steps, slab, 3, width).transpose(0, 2, 1, 3)
    q0, k0, v0, q1, k1, v1 = spread(projected.reshape(steps * 3, slab, width))
    fresh_all = gather(jnp.stack([k0, v0]))
    outs = jnp.stack(
        [attend(ring, slab, q0, stale_all, k0, v0), attend(ring, slab, q1, fresh_all, k1, v1)]
    )
    if group > 1:
        back = outs.reshape(steps, group, slab, part).transpose(1, 0, 2, 3)
        back = lax.all_to_all(back, "patch", 0, 0, axis_index_groups=columns, tiled=True)
        outs = back.transpose(1, 2, 0, 3).reshape(steps, slab, width)
    return finish(outs.reshape(steps * slab, width), hidden, attn_gate, w_out)


def solution(mesh):
    in_specs = (
        P(None, "patch", "head"),
        P(None, "patch", "head"),
        P(),
        P(None, "head"),
        P(None, None, "head"),
        P("head", None),
    )
    return jax.shard_map(
        functools.partial(on_device, mesh.shape["patch"]),
        mesh=mesh,
        in_specs=in_specs,
        out_specs=P(None, "patch", "head"),
        check_vma=False,
    )
```

```python
import functools
import math

import jax
import jax.numpy as jnp
from jax import lax
from jax.experimental import pallas as pl
from jax.experimental.pallas import tpu as pltpu
from jax.sharding import PartitionSpec as P

HEAD_DIM = 128
SCALE = HEAD_DIM ** (-0.5) * math.log2(math.e)


def layer_norm(values_in):
    mean_value = jnp.mean(values_in, axis=-1, keepdims=True)
    centred = values_in - mean_value
    variance = jnp.mean(centred * centred, axis=-1, keepdims=True)
    return centred * lax.rsqrt(variance + 1e-06)


def attend_kernel(ring, slab, q_ref, k_ref, v_ref, kf_ref, vf_ref, o_ref, kbuf, vbuf):
    mine = lax.rem(lax.axis_index("patch"), ring)
    group = q_ref.shape[0] // slab
    kbuf[...] = k_ref[:, 0]
    vbuf[...] = v_ref[:, 0]

    def one_slab(j, carry):
        rows = pl.ds(pl.multiple_of(j * slab, slab), slab)
        here = pl.ds(mine, 1)
        kbuf[here, rows] = kf_ref[rows][None]
        vbuf[here, rows] = vf_ref[rows][None]
        keys = kbuf[...].reshape(ring * group * slab, HEAD_DIM)
        values = vbuf[...].reshape(ring * group * slab, HEAD_DIM)
        scores = lax.dot_general(
            q_ref[rows], keys, (((1,), (1,)), ((), ())), preferred_element_type=jnp.float32
        )
        peak = jnp.max(scores, axis=-1, keepdims=True)
        weights = jnp.exp2((scores - peak) * SCALE)
        total = jnp.sum(weights, axis=-1, keepdims=True)
        summed = jnp.dot(weights.astype(jnp.bfloat16), values, preferred_element_type=jnp.float32)
        o_ref[rows] = (summed / total).astype(jnp.bfloat16)
        kbuf[here, rows] = k_ref[here, 0, rows]
        vbuf[here, rows] = v_ref[here, 0, rows]
        return carry

    lax.fori_loop(0, group, one_slab, 0)


def attend(ring, slab, queries, gathered, fresh_keys, fresh_values):
    rows, width = queries.shape
    heads = width // HEAD_DIM
    flat = pl.BlockSpec((rows, HEAD_DIM), lambda h: (0, h))
    return pl.pallas_call(
        functools.partial(attend_kernel, ring, slab),
        grid=(heads,),
        out_shape=jax.ShapeDtypeStruct((rows, width), jnp.bfloat16),
        in_specs=[
            flat,
            pl.BlockSpec((ring, 1, rows, HEAD_DIM), lambda h: (0, 0, 0, h)),
            pl.BlockSpec((ring, 1, rows, HEAD_DIM), lambda h: (0, 1, 0, h)),
            flat,
            flat,
        ],
        out_specs=flat,
        scratch_shapes=[
            pltpu.VMEM((ring, rows, HEAD_DIM), jnp.bfloat16),
            pltpu.VMEM((ring, rows, HEAD_DIM), jnp.bfloat16),
        ],
        compiler_params=pltpu.CompilerParams(vmem_limit_bytes=48 * 2**20),
        cost_estimate=pl.CostEstimate(
            flops=4 * rows * width * rows * ring,
            bytes_accessed=2 * width * rows * (2 * ring + 4),
            transcendentals=rows * rows * ring * heads,
        ),
    )(queries, gathered, gathered, fresh_keys, fresh_values)


K0, V0, Q0, Q1, K1, V1, SK, SV = range(8)
PLACE = {K0: (1, 0), V0: (2, 0), Q0: (0, 0), Q1: (0, 1), K1: (1, 1), V1: (2, 1)}
PLANE = {SK: 0, SV: 1, K0: 2, V0: 3}
TILE = 256
MESH = pl.DeviceIdType.MESH


def attend_step(query, fresh_k, fresh_v, own, others, kbuf, vbuf, store):
    group, slab, _ = kbuf.shape
    kbuf[...], vbuf[...] = own()

    def one_slot(j, carry):
        here = pl.ds(j, 1)
        kept_k, kept_v = kbuf[here], vbuf[here]
        kbuf[here] = fresh_k(here)
        vbuf[here] = fresh_v(here)
        rows = query(here).reshape(slab, HEAD_DIM)
        blocks = [(kbuf[...], vbuf[...])] + [other() for other in others]
        blocks = [[part.reshape(group * slab, HEAD_DIM) for part in block] for block in blocks]
        scores = [
            lax.dot_general(rows, k, (((1,), (1,)), ((), ())), preferred_element_type=jnp.float32)
            for k, _ in blocks
        ]
        peak = functools.reduce(
            jnp.maximum, [jnp.max(block, axis=-1, keepdims=True) for block in scores]
        )
        total, summed = 0.0, 0.0
        for block, (_, v) in zip(scores, blocks):
            weights = jnp.exp2((block - peak) * SCALE)
            total += jnp.sum(weights, axis=-1, keepdims=True)
            summed += jnp.dot(weights.astype(jnp.bfloat16), v, preferred_element_type=jnp.float32)
        store(here, (summed / total).astype(jnp.bfloat16)[None])
        kbuf[here] = kept_k
        vbuf[here] = kept_v
        return carry

    lax.fori_loop(0, group, one_slot, 0)


def block_kernel(
    ring, hidden_ref, stale_ref, mod_ref, gate_ref, w_qkv_ref, w_out_ref, updated_ref,
    hid, normed, w_buf, proj, col, gath, out, att, w_out, give, take, kbuf, vbuf,
    z_send, z_recv, loc_sem, f_send, f_recv, o_send, o_recv, w_sem, w_out_sem, hid_sem, p_send, p_recv,
):
    me, core = lax.axis_index("patch"), lax.axis_index("head")
    z, p = lax.div(me, ring), lax.rem(me, ring)
    _, group, slab, part = col.shape
    _, steps, _, width = hid.shape
    heads = part // HEAD_DIM

    def column_peer(d):
        return {"patch": lax.rem(z + d + group, group) * ring + p}

    beside = {"patch": z * ring + p + 1 - 2 * lax.rem(p, 2)}
    above = {"patch": z * ring + lax.rem(p + 2, 4)}
    twin = {"head": 1 - core}
    barrier = pltpu.get_barrier_semaphore()
    greeted = [column_peer(d) for d in range(1, group)] + [beside, above]
    for peer in greeted + [twin]:
        pl.semaphore_signal(barrier, inc=1, device_id=peer, device_id_type=MESH)

    def weight_copy(n):
        which, half = (1, 2, 0)[n // 2], n % 2
        columns = pl.ds(half * (width // 2), width // 2)
        return pltpu.make_async_copy(
            w_qkv_ref.at[which, :, columns], w_buf.at[n % 2], w_sem.at[n % 2]
        )

    weight_copy(0).start()
    weight_copy(1).start()
    hid_own = pltpu.make_async_copy(hidden_ref, hid.at[core], hid_sem.at[0])
    hid_own.start()
    pl.semaphore_wait(barrier, group + 2)
    hid_swap = pltpu.make_async_remote_copy(
        src_ref=hidden_ref, dst_ref=hid.at[core], send_sem=hid_sem.at[1], recv_sem=hid_sem.at[2],
        device_id=twin, device_id_type=MESH,
    )
    hid_swap.start()

    def source(a, owner):
        columns = pl.ds(pl.multiple_of(owner * part, part), part)
        if a in (SK, SV):
            return stale_ref.at[a - SK, :, columns]
        which, step = PLACE[a]
        return proj.at[which, pl.ds(step * slab, slab), columns]

    moves = {}

    def spread(arrays):
        for a in arrays:
            moves[a, 0] = pltpu.make_async_copy(source(a, z), col.at[a, 0], loc_sem.at[a])
            moves[a, 0].start()
        for d in range(1, group):
            for a in arrays:
                moves[a, d] = pltpu.make_async_remote_copy(
                    src_ref=source(a, lax.rem(z + d, group)),
                    dst_ref=col.at[a, d],
                    send_sem=z_send.at[a, d],
                    recv_sem=z_recv.at[a, d],
                    device_id=column_peer(d),
                    device_id_type=MESH,
                )
                moves[a, d].start()

    def arrive(a, d):
        if d == 0:
            moves[a, 0].wait()
        else:
            moves[a, d].wait_recv()

    forwards = {}

    def send_plane(a, d, e, src, peer):
        slot = PLANE[a]
        forwards[a, d, e] = pltpu.make_async_remote_copy(
            src_ref=src,
            dst_ref=gath.at[slot, e, d],
            send_sem=f_send.at[slot, d, e],
            recv_sem=f_recv.at[slot, d, e],
            device_id=peer,
            device_id_type=MESH,
        )
        forwards[a, d, e].start()

    def forward(pair, d):
        for a in pair:
            arrive(a, d)
            send_plane(a, d, 0, col.at[a, d], beside)
            send_plane(a, d, 1, col.at[a, d], above)

    def relay(pair, d):
        for a, e, peer in ((pair[0], 1, beside), (pair[1], 0, above)):
            forwards[a, d, e].wait_recv()
            relayed.add((a, d, e))
            send_plane(a, d, 2, gath.at[PLANE[a], e, d], peer)

    relayed = set()
    stale, past = (SK, SV), (K0, V0)
    spread((SK, SV))
    forward(stale, 0)
    hid_own.wait()
    hid_swap.wait_recv()

    block = slab // 4

    def norm_rows(n, carry):
        step = lax.div(n, 4)
        rows = pl.ds(pl.multiple_of(lax.rem(n, 4) * block, block), block)
        here = pl.ds(step, 1)
        halves = [hid[c, here, rows].reshape(block, width).astype(jnp.float32) for c in range(2)]
        count = 2 * width
        mean_value = sum(jnp.sum(half, axis=-1, keepdims=True) for half in halves) / count
        centred = [half - mean_value for half in halves]
        variance = sum(jnp.sum(half * half, axis=-1, keepdims=True) for half in centred) / count
        inverse = lax.rsqrt(variance + 1e-06)
        landing = pl.ds(pl.multiple_of(n * block, block), block)
        for c in range(2):
            lanes = pl.ds(c * width, width)
            shift = mod_ref[here, 0, lanes].reshape(1, width)
            scale = mod_ref[here, 1, lanes].reshape(1, width)
            value = centred[c] * inverse * (1.0 + scale) + shift
            normed[landing, lanes] = value.astype(jnp.bfloat16)
        return carry

    lax.fori_loop(0, 4 * steps, norm_rows, 0)

    def project(n):
        which, half = (1, 2, 0)[n // 2], n % 2
        weight_copy(n).wait()

        def tile(t, carry):
            lanes = pl.ds(pl.multiple_of(t * TILE, TILE), TILE)
            landing = pl.ds(pl.multiple_of(half * (width // 2) + t * TILE, TILE), TILE)
            value = jnp.dot(normed[...], w_buf[n % 2, :, lanes], preferred_element_type=jnp.float32)
            proj[which, :, landing] = value.astype(jnp.bfloat16)
            return carry

        lax.fori_loop(0, width // 2 // TILE, tile, 0)
        if n + 2 < 6:
            weight_copy(n + 2).start()

    project(0)
    project(1)
    spread((K0,))
    forward(stale, 1)
    relay(stale, 0)
    project(2)
    project(3)
    spread((V0,))
    forward(stale, 2)
    relay(stale, 1)
    project(4)
    project(5)
    spread((Q0,))
    spread((Q1,))
    spread((K1, V1))
    w_out_copies = []
    for side in range(2):
        half = 1 - core if side == 0 else core
        columns = pl.ds(pl.multiple_of(half * width, width), width)
        w_out_copies.append(
            pltpu.make_async_copy(w_out_ref.at[:, columns], w_out.at[side], w_out_sem.at[side])
        )
        w_out_copies[side].start()
    forward(stale, 3)
    relay(stale, 2)
    forward(past, 0)
    relay(stale, 3)
    forward(past, 1)
    relay(past, 0)
    forward(past, 2)
    relay(past, 1)
    forward(past, 3)

    returns = {}

    def run_step(step, query_a, key_a, value_a, past_k, past_v, between):
        for h in range(heads):
            lanes = pl.ds(h * HEAD_DIM, HEAD_DIM)

            def store(here, value):
                out[step, h, here] = value

            attend_step(
                lambda here: col[query_a, here, :, lanes],
                lambda here: col[key_a, here, :, lanes],
                lambda here: col[value_a, here, :, lanes],
                lambda: (col[past_k, :, :, lanes], col[past_v, :, :, lanes]),
                [
                    lambda e=e: (
                        gath[PLANE[past_k], e, :, :, lanes],
                        gath[PLANE[past_v], e, :, :, lanes],
                    )
                    for e in range(3)
                ],
                kbuf, vbuf, store,
            )
            columns = pl.ds(pl.multiple_of(z * part + h * HEAD_DIM, HEAD_DIM), HEAD_DIM)
            landing = att.at[step, :, columns]
            for j in range(group):
                if j == 0:
                    back = pltpu.make_async_copy(out.at[step, h, 0], landing, o_recv.at[step, h, 0])
                else:
                    back = pltpu.make_async_remote_copy(
                        src_ref=out.at[step, h, j],
                        dst_ref=landing,
                        send_sem=o_send.at[step, h, j],
                        recv_sem=o_recv.at[step, h, j],
                        device_id=column_peer(-j),
                        device_id_type=MESH,
                    )
                back.start()
                returns[step, h, j] = back
            between(h)

    def wait_plane(arrays):
        for key, copy in forwards.items():
            if key[0] in arrays and key not in relayed:
                copy.wait_recv()

    def branch_tile(step, side, t):
        lanes = pl.ds(pl.multiple_of(t * TILE, TILE), TILE)
        return lanes, jnp.dot(att[step], w_out[side, :, lanes], preferred_element_type=jnp.float32)

    def share(step):
        for back in [copy for key, copy in returns.items() if key[0] == step]:
            back.wait()

        def tile(t, carry):
            lanes, value = branch_tile(step, 0, t)
            give[step, :, lanes] = value.astype(jnp.bfloat16)
            return carry

        lax.fori_loop(0, width // TILE, tile, 0)
        copy = pltpu.make_async_remote_copy(
            src_ref=give.at[step], dst_ref=take.at[step],
            send_sem=p_send.at[step], recv_sem=p_recv.at[step],
            device_id=twin, device_id_type=MESH,
        )
        copy.start()
        return copy

    def update(step, copy):
        copy.wait_recv()

        def tile(t, carry):
            lanes, value = branch_tile(step, 1, t)
            value = value + take[step, :, lanes].astype(jnp.float32)
            before = hid[pl.ds(core, 1), step, :, lanes].reshape(slab, TILE).astype(jnp.float32)
            after = before + gate_ref[pl.ds(step, 1), lanes] * value
            updated_ref[step, :, lanes] = after.astype(jnp.bfloat16)
            return carry

        lax.fori_loop(0, width // TILE, tile, 0)

    for d in range(group):
        arrive(Q0, d)
    wait_plane((SK, SV))
    run_step(0, Q0, K0, V0, SK, SV, lambda h: relay(past, h + 2) if h < 2 else None)
    for a in (Q1, K1, V1):
        for d in range(group):
            arrive(a, d)
    wait_plane((K0, V0))
    run_step(1, Q1, K1, V1, K0, V0, lambda h: None)
    for copy in w_out_copies:
        copy.wait()
    shares = [share(step) for step in range(steps)]
    for step in range(steps):
        update(step, shares[step])
    for copy in shares + [hid_swap] + list(forwards.values()):
        copy.wait_send()
    for (_, d), copy in moves.items():
        if d > 0:
            copy.wait_send()


def whole_block(group, ring, hidden, stale_kv, modulation, attn_gate, w_qkv, w_out):
    steps, slab, width = hidden.shape
    part = width // group
    heads = part // HEAD_DIM
    bf16, dma = jnp.bfloat16, pltpu.SemaphoreType.DMA
    vmem, anywhere = pl.BlockSpec(memory_space=pltpu.VMEM), pl.BlockSpec(memory_space=pl.ANY)
    return pl.pallas_call(
        functools.partial(block_kernel, ring),
        out_shape=jax.ShapeDtypeStruct(hidden.shape, bf16),
        in_specs=[anywhere, anywhere, vmem, vmem, anywhere, anywhere],
        out_specs=vmem,
        scratch_shapes=[
            pltpu.VMEM((2, steps, slab, width), bf16),
            pltpu.VMEM((steps * slab, 2 * width), bf16),
            pltpu.VMEM((2, 2 * width, width // 2), bf16),
            pltpu.VMEM((3, steps * slab, width), bf16),
            pltpu.VMEM((8, group, slab, part), bf16),
            pltpu.VMEM((4, 3, group, slab, part), bf16),
            pltpu.VMEM((steps, heads, group, slab, HEAD_DIM), bf16),
            pltpu.VMEM((steps, slab, width), bf16),
            pltpu.VMEM((2, width, width), bf16),
            pltpu.VMEM((steps, slab, width), bf16),
            pltpu.VMEM((steps, slab, width), bf16),
            pltpu.VMEM((group, slab, HEAD_DIM), bf16),
            pltpu.VMEM((group, slab, HEAD_DIM), bf16),
            dma((8, group)),
            dma((8, group)),
            dma((8,)),
            dma((4, group, 3)),
            dma((4, group, 3)),
            dma((steps, heads, group)),
            dma((steps, heads, group)),
            dma((2,)),
            dma((2,)),
            dma((3,)),
            dma((steps,)),
            dma((steps,)),
        ],
        compiler_params=pltpu.CompilerParams(
            collective_id=0, has_side_effects=True, vmem_limit_bytes=60 * 2**20
        ),
        cost_estimate=pl.CostEstimate(
            flops=steps * slab * width * (16 * width + 4 * slab * group * ring),
            bytes_accessed=2 * width * (8 * width + 6 * steps * slab),
            transcendentals=steps * slab * slab * group * ring * width // HEAD_DIM,
        ),
    )(hidden, stale_kv, modulation, attn_gate, jnp.transpose(w_qkv, (1, 0, 2)), w_out)


def finish(outs, hidden, attn_gate, w_out):
    partial_out = jnp.dot(outs, w_out, preferred_element_type=jnp.float32)
    branch = lax.psum_scatter(
        partial_out.astype(jnp.bfloat16), "head", scatter_dimension=1, tiled=True
    ).astype(jnp.float32)
    gated = attn_gate[:, None] * branch.reshape(hidden.shape)
    return (hidden.astype(jnp.float32) + gated).astype(jnp.bfloat16)


def on_device(patches, hidden, stale_kv, modulation, attn_gate, w_qkv, w_out):
    steps, slab, width = hidden.shape
    group = math.gcd(width // HEAD_DIM, patches)
    ring = patches // group
    if group == 4 and ring == 4 and steps == 2 and w_out.shape[1] == 2 * width:
        return whole_block(group, ring, hidden, stale_kv, modulation, attn_gate, w_qkv, w_out)
    columns = [[g * ring + p for g in range(group)] for p in range(ring)]
    planes = [[g * ring + p for p in range(ring)] for g in range(group)]
    part = width // group

    def spread(rows):
        n = rows.shape[0]
        if group == 1:
            return rows
        split = rows.reshape(n, slab, group, part).transpose(2, 0, 1, 3)
        got = lax.all_to_all(split, "patch", 0, 0, axis_index_groups=columns, tiled=True)
        return got.transpose(1, 0, 2, 3).reshape(n, group * slab, part)

    def gather(rows):
        return lax.all_gather(rows, "patch", axis=0, axis_index_groups=planes)

    stale_all = gather(spread(stale_kv))
    full_rows = lax.all_gather(hidden, "head", axis=2, tiled=True)
    normed = layer_norm(full_rows.astype(jnp.float32))
    normed = (normed * (1.0 + modulation[:, 1][:, None]) + modulation[:, 0][:, None]).astype(
        jnp.bfloat16
    )
    projected = jnp.dot(
        normed.reshape(steps * slab, -1),
        w_qkv.reshape(w_qkv.shape[0], -1),
        preferred_element_type=jnp.float32,
    ).astype(jnp.bfloat16)
    projected = projected.reshape(steps, slab, 3, width).transpose(0, 2, 1, 3)
    q0, k0, v0, q1, k1, v1 = spread(projected.reshape(steps * 3, slab, width))
    fresh_all = gather(jnp.stack([k0, v0]))
    outs = jnp.stack(
        [attend(ring, slab, q0, stale_all, k0, v0), attend(ring, slab, q1, fresh_all, k1, v1)]
    )
    if group > 1:
        back = outs.reshape(steps, group, slab, part).transpose(1, 0, 2, 3)
        back = lax.all_to_all(back, "patch", 0, 0, axis_index_groups=columns, tiled=True)
        outs = back.transpose(1, 2, 0, 3).reshape(steps, slab, width)
    return finish(outs.reshape(steps * slab, width), hidden, attn_gate, w_out)


def solution(mesh):
    in_specs = (
        P(None, "patch", "head"),
        P(None, "patch", "head"),
        P(),
        P(None, "head"),
        P(None, None, "head"),
        P("head", None),
    )
    return jax.shard_map(
        functools.partial(on_device, mesh.shape["patch"]),
        mesh=mesh,
        in_specs=in_specs,
        out_specs=P(None, "patch", "head"),
        check_vma=False,
    )
```

```python
import functools
import math

import jax
import jax.numpy as jnp
from jax import lax
from jax.experimental import pallas as pl
from jax.experimental.pallas import tpu as pltpu
from jax.sharding import PartitionSpec as P

HEAD_DIM = 128
SCALE = HEAD_DIM ** (-0.5) * math.log2(math.e)


def layer_norm(values_in):
    mean_value = jnp.mean(values_in, axis=-1, keepdims=True)
    centred = values_in - mean_value
    variance = jnp.mean(centred * centred, axis=-1, keepdims=True)
    return centred * lax.rsqrt(variance + 1e-06)


def attend_kernel(ring, slab, q_ref, k_ref, v_ref, kf_ref, vf_ref, o_ref, kbuf, vbuf):
    mine = lax.rem(lax.axis_index("patch"), ring)
    group = q_ref.shape[0] // slab
    kbuf[...] = k_ref[:, 0]
    vbuf[...] = v_ref[:, 0]

    def one_slab(j, carry):
        rows = pl.ds(pl.multiple_of(j * slab, slab), slab)
        here = pl.ds(mine, 1)
        kbuf[here, rows] = kf_ref[rows][None]
        vbuf[here, rows] = vf_ref[rows][None]
        keys = kbuf[...].reshape(ring * group * slab, HEAD_DIM)
        values = vbuf[...].reshape(ring * group * slab, HEAD_DIM)
        scores = lax.dot_general(
            q_ref[rows], keys, (((1,), (1,)), ((), ())), preferred_element_type=jnp.float32
        )
        peak = jnp.max(scores, axis=-1, keepdims=True)
        weights = jnp.exp2((scores - peak) * SCALE)
        total = jnp.sum(weights, axis=-1, keepdims=True)
        summed = jnp.dot(weights.astype(jnp.bfloat16), values, preferred_element_type=jnp.float32)
        o_ref[rows] = (summed / total).astype(jnp.bfloat16)
        kbuf[here, rows] = k_ref[here, 0, rows]
        vbuf[here, rows] = v_ref[here, 0, rows]
        return carry

    lax.fori_loop(0, group, one_slab, 0)


def attend(ring, slab, queries, gathered, fresh_keys, fresh_values):
    rows, width = queries.shape
    heads = width // HEAD_DIM
    flat = pl.BlockSpec((rows, HEAD_DIM), lambda h: (0, h))
    return pl.pallas_call(
        functools.partial(attend_kernel, ring, slab),
        grid=(heads,),
        out_shape=jax.ShapeDtypeStruct((rows, width), jnp.bfloat16),
        in_specs=[
            flat,
            pl.BlockSpec((ring, 1, rows, HEAD_DIM), lambda h: (0, 0, 0, h)),
            pl.BlockSpec((ring, 1, rows, HEAD_DIM), lambda h: (0, 1, 0, h)),
            flat,
            flat,
        ],
        out_specs=flat,
        scratch_shapes=[
            pltpu.VMEM((ring, rows, HEAD_DIM), jnp.bfloat16),
            pltpu.VMEM((ring, rows, HEAD_DIM), jnp.bfloat16),
        ],
        compiler_params=pltpu.CompilerParams(vmem_limit_bytes=48 * 2**20),
        cost_estimate=pl.CostEstimate(
            flops=4 * rows * width * rows * ring,
            bytes_accessed=2 * width * rows * (2 * ring + 4),
            transcendentals=rows * rows * ring * heads,
        ),
    )(queries, gathered, gathered, fresh_keys, fresh_values)


K0, V0, Q0, Q1, SK, SV = range(6)
PLACE = {K0: (1, 0), V0: (2, 0), Q0: (0, 0), Q1: (0, 1)}
PLANE = {SK: 0, SV: 1, K0: 2, V0: 3}
TILE = 256
MESH = pl.DeviceIdType.MESH


def attend_step(query, fresh_k, fresh_v, own, others, kbuf, vbuf, store):
    group, slab, _ = kbuf.shape
    kbuf[...], vbuf[...] = own()

    def one_slot(j, carry):
        here = pl.ds(j, 1)
        kept_k, kept_v = kbuf[here], vbuf[here]
        kbuf[here] = fresh_k(here)
        vbuf[here] = fresh_v(here)
        rows = query(here).reshape(slab, HEAD_DIM)
        blocks = [(kbuf[...], vbuf[...])] + [other() for other in others]
        blocks = [[part.reshape(group * slab, HEAD_DIM) for part in block] for block in blocks]
        scores = [
            lax.dot_general(rows, k, (((1,), (1,)), ((), ())), preferred_element_type=jnp.float32)
            for k, _ in blocks
        ]
        peak = functools.reduce(
            jnp.maximum, [jnp.max(block, axis=-1, keepdims=True) for block in scores]
        )
        total, summed = 0.0, 0.0
        for block, (_, v) in zip(scores, blocks):
            weights = jnp.exp2((block - peak) * SCALE)
            total += jnp.sum(weights, axis=-1, keepdims=True)
            summed += jnp.dot(weights.astype(jnp.bfloat16), v, preferred_element_type=jnp.float32)
        store(here, (summed / total).astype(jnp.bfloat16)[None])
        kbuf[here] = kept_k
        vbuf[here] = kept_v
        return carry

    lax.fori_loop(0, group, one_slot, 0)


def weigh(rows, blocks):
    scores = [
        lax.dot_general(rows, k, (((1,), (1,)), ((), ())), preferred_element_type=jnp.float32)
        for k, _ in blocks
    ]
    peak = functools.reduce(
        jnp.maximum, [jnp.max(block, axis=-1, keepdims=True) for block in scores]
    )
    total, summed = 0.0, 0.0
    for block, (_, v) in zip(scores, blocks):
        weights = jnp.exp2((block - peak) * SCALE)
        total += jnp.sum(weights, axis=-1, keepdims=True)
        summed += jnp.dot(weights.astype(jnp.bfloat16), v, preferred_element_type=jnp.float32)
    return summed / total, peak * SCALE + jnp.log2(total)


def block_kernel(
    ring, hidden_ref, stale_ref, mod_ref, gate_ref, w_qkv_ref, w_out_ref, updated_ref,
    hid, normed, w_buf, proj, col, gath, out, att, w_out, give, take, kbuf, vbuf,
    near, near_level, level, level_out, level_in,
    z_send, z_recv, loc_sem, f_send, f_recv, o_send, o_recv, w_sem, w_out_sem, hid_sem, p_send, p_recv,
    l_send, l_recv,
):
    me, core = lax.axis_index("patch"), lax.axis_index("head")
    z, p = lax.div(me, ring), lax.rem(me, ring)
    _, group, slab, part = col.shape
    _, steps, _, width = hid.shape
    heads = part // HEAD_DIM

    def column_peer(d):
        return {"patch": lax.rem(z + d + group, group) * ring + p}

    beside = {"patch": z * ring + p + 1 - 2 * lax.rem(p, 2)}
    above = {"patch": z * ring + lax.rem(p + 2, 4)}
    twin = {"head": 1 - core}
    barrier = pltpu.get_barrier_semaphore()
    greeted = [column_peer(d) for d in range(1, group)] + [beside, above]
    for peer in greeted + [twin]:
        pl.semaphore_signal(barrier, inc=1, device_id=peer, device_id_type=MESH)

    def weight_copy(n):
        which, half = (1, 2, 0)[n // 2], n % 2
        columns = pl.ds(half * (width // 2), width // 2)
        return pltpu.make_async_copy(
            w_qkv_ref.at[which, :, columns], w_buf.at[n % 2], w_sem.at[n % 2]
        )

    weight_copy(0).start()
    weight_copy(1).start()
    hid_own = pltpu.make_async_copy(hidden_ref, hid.at[core], hid_sem.at[0])
    hid_own.start()
    pl.semaphore_wait(barrier, group + 2)
    hid_swap = pltpu.make_async_remote_copy(
        src_ref=hidden_ref, dst_ref=hid.at[core], send_sem=hid_sem.at[1], recv_sem=hid_sem.at[2],
        device_id=twin, device_id_type=MESH,
    )
    hid_swap.start()

    def source(a, owner):
        columns = pl.ds(pl.multiple_of(owner * part, part), part)
        if a in (SK, SV):
            return stale_ref.at[a - SK, :, columns]
        which, step = PLACE[a]
        return proj.at[which, pl.ds(step * slab, slab), columns]

    moves = {}

    def spread(arrays):
        for a in arrays:
            moves[a, 0] = pltpu.make_async_copy(source(a, z), col.at[a, 0], loc_sem.at[a])
            moves[a, 0].start()
        for d in range(1, group):
            for a in arrays:
                moves[a, d] = pltpu.make_async_remote_copy(
                    src_ref=source(a, lax.rem(z + d, group)),
                    dst_ref=col.at[a, d],
                    send_sem=z_send.at[a, d],
                    recv_sem=z_recv.at[a, d],
                    device_id=column_peer(d),
                    device_id_type=MESH,
                )
                moves[a, d].start()

    def arrive(a, d):
        if d == 0:
            moves[a, 0].wait()
        else:
            moves[a, d].wait_recv()

    forwards = {}

    def send_plane(a, d, e, src, peer):
        slot = PLANE[a]
        forwards[a, d, e] = pltpu.make_async_remote_copy(
            src_ref=src,
            dst_ref=gath.at[slot, e, d],
            send_sem=f_send.at[slot, d, e],
            recv_sem=f_recv.at[slot, d, e],
            device_id=peer,
            device_id_type=MESH,
        )
        forwards[a, d, e].start()

    def forward(pair, d):
        for a in pair:
            arrive(a, d)
            send_plane(a, d, 0, col.at[a, d], beside)
            send_plane(a, d, 1, col.at[a, d], above)

    def relay(pair, d):
        for a, e, peer in ((pair[0], 1, beside), (pair[1], 0, above)):
            forwards[a, d, e].wait_recv()
            relayed.add((a, d, e))
            send_plane(a, d, 2, gath.at[PLANE[a], e, d], peer)

    relayed = set()
    stale, past = (SK, SV), (K0, V0)
    spread((SK, SV))
    forward(stale, 0)
    hid_own.wait()
    hid_swap.wait_recv()

    block = slab // 4

    def norm_rows(n, carry):
        step = lax.div(n, 4)
        rows = pl.ds(pl.multiple_of(lax.rem(n, 4) * block, block), block)
        here = pl.ds(step, 1)
        halves = [hid[c, here, rows].reshape(block, width).astype(jnp.float32) for c in range(2)]
        count = 2 * width
        mean_value = sum(jnp.sum(half, axis=-1, keepdims=True) for half in halves) / count
        centred = [half - mean_value for half in halves]
        variance = sum(jnp.sum(half * half, axis=-1, keepdims=True) for half in centred) / count
        inverse = lax.rsqrt(variance + 1e-06)
        landing = pl.ds(pl.multiple_of(n * block, block), block)
        for c in range(2):
            lanes = pl.ds(c * width, width)
            shift = mod_ref[here, 0, lanes].reshape(1, width)
            scale = mod_ref[here, 1, lanes].reshape(1, width)
            value = centred[c] * inverse * (1.0 + scale) + shift
            normed[landing, lanes] = value.astype(jnp.bfloat16)
        return carry

    lax.fori_loop(0, 4 * steps, norm_rows, 0)

    def project(n):
        which, half = (1, 2, 0)[n // 2], n % 2
        weight_copy(n).wait()

        def tile(t, carry):
            lanes = pl.ds(pl.multiple_of(t * TILE, TILE), TILE)
            landing = pl.ds(pl.multiple_of(half * (width // 2) + t * TILE, TILE), TILE)
            value = jnp.dot(normed[...], w_buf[n % 2, :, lanes], preferred_element_type=jnp.float32)
            proj[which, :, landing] = value.astype(jnp.bfloat16)
            return carry

        lax.fori_loop(0, width // 2 // TILE, tile, 0)
        if n + 2 < 6:
            weight_copy(n + 2).start()

    project(0)
    project(1)
    spread((K0,))
    forward(stale, 1)
    relay(stale, 0)
    project(2)
    project(3)
    spread((V0,))
    forward(stale, 2)
    relay(stale, 1)
    project(4)
    project(5)
    spread((Q0,))
    spread((Q1,))
    w_out_copies = []
    for side in range(2):
        half = 1 - core if side == 0 else core
        columns = pl.ds(pl.multiple_of(half * width, width), width)
        w_out_copies.append(
            pltpu.make_async_copy(w_out_ref.at[:, columns], w_out.at[side], w_out_sem.at[side])
        )
        w_out_copies[side].start()
    forward(stale, 3)
    relay(stale, 2)
    forward(past, 0)
    relay(stale, 3)
    forward(past, 1)
    relay(past, 0)
    forward(past, 2)
    relay(past, 1)
    forward(past, 3)

    def attend_near(h, carry):
        lanes = pl.ds(pl.multiple_of(h * HEAD_DIM, HEAD_DIM), HEAD_DIM)
        rows = pl.ds(slab, slab)
        value, weight = weigh(proj[0, rows, lanes], [(proj[1, rows, lanes], proj[2, rows, lanes])])
        near[pl.ds(h, 1)] = value[None]
        near_level[pl.ds(h, 1)] = jnp.broadcast_to(weight, (slab, HEAD_DIM))[None]
        return carry

    lax.fori_loop(0, width // HEAD_DIM, attend_near, 0)
    level[...] = jnp.zeros_like(level)

    returns = {}

    def attend_far(h, lanes, e_slots):
        def one_slot(j, carry):
            def block(ref, a):
                rest = [ref[a, pl.ds(lax.rem(j + i, group), 1), :, lanes] for i in range(1, group)]
                return jnp.concatenate(rest, axis=0).reshape((group - 1) * slab, HEAD_DIM)

            blocks = [(block(col, K0), block(col, V0))]
            for e in e_slots:
                blocks.append(
                    tuple(
                        gath[PLANE[a], e, :, :, lanes].reshape(group * slab, HEAD_DIM)
                        for a in (K0, V0)
                    )
                )
            here = pl.ds(j, 1)
            value, weight = weigh(col[Q1, here, :, lanes].reshape(slab, HEAD_DIM), blocks)
            out[1, h, here] = value.astype(jnp.bfloat16)[None]
            places = lax.broadcasted_iota(jnp.int32, (slab, HEAD_DIM), 1)
            held = level[here, 0:slab].reshape(slab, HEAD_DIM)
            level[here, 0:slab] = jnp.where(places == h, weight, held)[None]
            return carry

        lax.fori_loop(0, group, one_slot, 0)

    levels = []

    def send_levels():
        for j in range(group):
            level_out[j] = jnp.transpose(level[j])[:8]
        for j in range(group):
            if j == 0:
                copy = pltpu.make_async_copy(level_out.at[0], level_in.at[z], l_recv.at[0])
            else:
                copy = pltpu.make_async_remote_copy(
                    src_ref=level_out.at[j], dst_ref=level_in.at[z],
                    send_sem=l_send.at[j], recv_sem=l_recv.at[j],
                    device_id=column_peer(-j), device_id_type=MESH,
                )
            copy.start()
            levels.append(copy)

    def merge():
        for back in [copy for key, copy in returns.items() if key[0] == 1] + levels:
            back.wait()
        for u in range(group):
            padded = jnp.concatenate(
                [level_in[u], jnp.zeros((HEAD_DIM - 8, level_in.shape[2]), jnp.float32)], axis=0
            )
            columns = jnp.transpose(padded)
            for h in range(heads):
                lanes = pl.ds(u * part + h * HEAD_DIM, HEAD_DIM)
                far_level = columns[:slab, h : h + 1]
                here_level = near_level[u * heads + h][:, :1]
                top = jnp.maximum(far_level, here_level)
                far_share, near_share = jnp.exp2(far_level - top), jnp.exp2(here_level - top)
                value = att[1, :, lanes].astype(jnp.float32) * far_share
                value = value + near[u * heads + h] * near_share
                att[1, :, lanes] = (value / (far_share + near_share)).astype(jnp.bfloat16)

    def run_step(step, query_a, key_a, value_a, past_k, past_v, between):
        for h in range(heads):
            lanes = pl.ds(h * HEAD_DIM, HEAD_DIM)

            def store(here, value):
                out[step, h, here] = value

            if step == 0:
                attend_step(
                    lambda here: col[query_a, here, :, lanes],
                    lambda here: col[key_a, here, :, lanes],
                    lambda here: col[value_a, here, :, lanes],
                    lambda: (col[past_k, :, :, lanes], col[past_v, :, :, lanes]),
                    [
                        lambda e=e: (
                            gath[PLANE[past_k], e, :, :, lanes],
                            gath[PLANE[past_v], e, :, :, lanes],
                        )
                        for e in range(3)
                    ],
                    kbuf, vbuf, store,
                )
            else:
                attend_far(h, lanes, range(3))
            columns = pl.ds(pl.multiple_of(z * part + h * HEAD_DIM, HEAD_DIM), HEAD_DIM)
            landing = att.at[step, :, columns]
            for j in range(group):
                if j == 0:
                    back = pltpu.make_async_copy(out.at[step, h, 0], landing, o_recv.at[step, h, 0])
                else:
                    back = pltpu.make_async_remote_copy(
                        src_ref=out.at[step, h, j],
                        dst_ref=landing,
                        send_sem=o_send.at[step, h, j],
                        recv_sem=o_recv.at[step, h, j],
                        device_id=column_peer(-j),
                        device_id_type=MESH,
                    )
                back.start()
                returns[step, h, j] = back
            between(h)

    def wait_plane(arrays):
        for key, copy in forwards.items():
            if key[0] in arrays and key not in relayed:
                copy.wait_recv()

    def branch_tile(step, side, t):
        lanes = pl.ds(pl.multiple_of(t * TILE, TILE), TILE)
        return lanes, jnp.dot(att[step], w_out[side, :, lanes], preferred_element_type=jnp.float32)

    def share(step):
        if step == 1:
            merge()
        else:
            for back in [copy for key, copy in returns.items() if key[0] == 0]:
                back.wait()

        def tile(t, carry):
            lanes, value = branch_tile(step, 0, t)
            give[step, :, lanes] = value.astype(jnp.bfloat16)
            return carry

        lax.fori_loop(0, width // TILE, tile, 0)
        copy = pltpu.make_async_remote_copy(
            src_ref=give.at[step], dst_ref=take.at[step],
            send_sem=p_send.at[step], recv_sem=p_recv.at[step],
            device_id=twin, device_id_type=MESH,
        )
        copy.start()
        return copy

    def update(step, copy):
        copy.wait_recv()

        def tile(t, carry):
            lanes, value = branch_tile(step, 1, t)
            value = value + take[step, :, lanes].astype(jnp.float32)
            before = hid[pl.ds(core, 1), step, :, lanes].reshape(slab, TILE).astype(jnp.float32)
            after = before + gate_ref[pl.ds(step, 1), lanes] * value
            updated_ref[step, :, lanes] = after.astype(jnp.bfloat16)
            return carry

        lax.fori_loop(0, width // TILE, tile, 0)

    for d in range(group):
        arrive(Q0, d)
    wait_plane((SK, SV))
    run_step(0, Q0, K0, V0, SK, SV, lambda h: relay(past, h + 2) if h < 2 else None)
    for d in range(group):
        arrive(Q1, d)
    wait_plane((K0, V0))
    run_step(1, Q1, K0, V0, K0, V0, lambda h: None)
    send_levels()
    for copy in w_out_copies:
        copy.wait()
    shares = [share(step) for step in range(steps)]
    for step in range(steps):
        update(step, shares[step])
    for copy in shares + [hid_swap] + list(forwards.values()):
        copy.wait_send()
    for (_, d), copy in moves.items():
        if d > 0:
            copy.wait_send()


def whole_block(group, ring, hidden, stale_kv, modulation, attn_gate, w_qkv, w_out):
    steps, slab, width = hidden.shape
    part = width // group
    heads = part // HEAD_DIM
    bf16, dma = jnp.bfloat16, pltpu.SemaphoreType.DMA
    vmem, anywhere = pl.BlockSpec(memory_space=pltpu.VMEM), pl.BlockSpec(memory_space=pl.ANY)
    return pl.pallas_call(
        functools.partial(block_kernel, ring),
        out_shape=jax.ShapeDtypeStruct(hidden.shape, bf16),
        in_specs=[anywhere, anywhere, vmem, vmem, anywhere, anywhere],
        out_specs=vmem,
        scratch_shapes=[
            pltpu.VMEM((2, steps, slab, width), bf16),
            pltpu.VMEM((steps * slab, 2 * width), bf16),
            pltpu.VMEM((2, 2 * width, width // 2), bf16),
            pltpu.VMEM((3, steps * slab, width), bf16),
            pltpu.VMEM((6, group, slab, part), bf16),
            pltpu.VMEM((4, 3, group, slab, part), bf16),
            pltpu.VMEM((steps, heads, group, slab, HEAD_DIM), bf16),
            pltpu.VMEM((steps, slab, width), bf16),
            pltpu.VMEM((2, width, width), bf16),
            pltpu.VMEM((steps, slab, width), bf16),
            pltpu.VMEM((steps, slab, width), bf16),
            pltpu.VMEM((group, slab, HEAD_DIM), bf16),
            pltpu.VMEM((group, slab, HEAD_DIM), bf16),
            pltpu.VMEM((width // HEAD_DIM, slab, HEAD_DIM), jnp.float32),
            pltpu.VMEM((width // HEAD_DIM, slab, HEAD_DIM), jnp.float32),
            pltpu.VMEM((group, 256, HEAD_DIM), jnp.float32),
            pltpu.VMEM((group, 8, 256), jnp.float32),
            pltpu.VMEM((group, 8, 256), jnp.float32),
            dma((6, group)),
            dma((6, group)),
            dma((6,)),
            dma((4, group, 3)),
            dma((4, group, 3)),
            dma((steps, heads, group)),
            dma((steps, heads, group)),
            dma((2,)),
            dma((2,)),
            dma((3,)),
            dma((steps,)),
            dma((steps,)),
            dma((group,)),
            dma((group,)),
        ],
        compiler_params=pltpu.CompilerParams(
            collective_id=0, has_side_effects=True, vmem_limit_bytes=60 * 2**20
        ),
        cost_estimate=pl.CostEstimate(
            flops=steps * slab * width * (16 * width + 4 * slab * group * ring),
            bytes_accessed=2 * width * (8 * width + 6 * steps * slab),
            transcendentals=steps * slab * slab * group * ring * width // HEAD_DIM,
        ),
    )(hidden, stale_kv, modulation, attn_gate, jnp.transpose(w_qkv, (1, 0, 2)), w_out)


def finish(outs, hidden, attn_gate, w_out):
    partial_out = jnp.dot(outs, w_out, preferred_element_type=jnp.float32)
    branch = lax.psum_scatter(
        partial_out.astype(jnp.bfloat16), "head", scatter_dimension=1, tiled=True
    ).astype(jnp.float32)
    gated = attn_gate[:, None] * branch.reshape(hidden.shape)
    return (hidden.astype(jnp.float32) + gated).astype(jnp.bfloat16)


def on_device(patches, hidden, stale_kv, modulation, attn_gate, w_qkv, w_out):
    steps, slab, width = hidden.shape
    group = math.gcd(width // HEAD_DIM, patches)
    ring = patches // group
    if group == 4 and ring == 4 and steps == 2 and slab <= 256 and w_out.shape[1] == 2 * width:
        return whole_block(group, ring, hidden, stale_kv, modulation, attn_gate, w_qkv, w_out)
    columns = [[g * ring + p for g in range(group)] for p in range(ring)]
    planes = [[g * ring + p for p in range(ring)] for g in range(group)]
    part = width // group

    def spread(rows):
        n = rows.shape[0]
        if group == 1:
            return rows
        split = rows.reshape(n, slab, group, part).transpose(2, 0, 1, 3)
        got = lax.all_to_all(split, "patch", 0, 0, axis_index_groups=columns, tiled=True)
        return got.transpose(1, 0, 2, 3).reshape(n, group * slab, part)

    def gather(rows):
        return lax.all_gather(rows, "patch", axis=0, axis_index_groups=planes)

    stale_all = gather(spread(stale_kv))
    full_rows = lax.all_gather(hidden, "head", axis=2, tiled=True)
    normed = layer_norm(full_rows.astype(jnp.float32))
    normed = (normed * (1.0 + modulation[:, 1][:, None]) + modulation[:, 0][:, None]).astype(
        jnp.bfloat16
    )
    projected = jnp.dot(
        normed.reshape(steps * slab, -1),
        w_qkv.reshape(w_qkv.shape[0], -1),
        preferred_element_type=jnp.float32,
    ).astype(jnp.bfloat16)
    projected = projected.reshape(steps, slab, 3, width).transpose(0, 2, 1, 3)
    q0, k0, v0, q1, k1, v1 = spread(projected.reshape(steps * 3, slab, width))
    fresh_all = gather(jnp.stack([k0, v0]))
    outs = jnp.stack(
        [attend(ring, slab, q0, stale_all, k0, v0), attend(ring, slab, q1, fresh_all, k1, v1)]
    )
    if group > 1:
        back = outs.reshape(steps, group, slab, part).transpose(1, 0, 2, 3)
        back = lax.all_to_all(back, "patch", 0, 0, axis_index_groups=columns, tiled=True)
        outs = back.transpose(1, 2, 0, 3).reshape(steps, slab, width)
    return finish(outs.reshape(steps * slab, width), hidden, attn_gate, w_out)


def solution(mesh):
    in_specs = (
        P(None, "patch", "head"),
        P(None, "patch", "head"),
        P(),
        P(None, "head"),
        P(None, None, "head"),
        P("head", None),
    )
    return jax.shard_map(
        functools.partial(on_device, mesh.shape["patch"]),
        mesh=mesh,
        in_specs=in_specs,
        out_specs=P(None, "patch", "head"),
        check_vma=False,
    )
```
